256 devices in a mesh: row: 4 (over x_lo, core), col: 16 (over z, x_hi), layer: 4 (over y).
Axes of the slice: x: 4 (x_hi: 2, x_lo: 2; x = x_hi * 2 + x_lo), y: 4, z: 8, core: 2. Of those that a mesh axis runs over, the one named last changes fastest.
Arguments:
- a_blocks: float32 [384, 12, 128, 128], P(('row', 'col'), 'layer'), may hold values from -0.5 to 0.5
- a_inner: int32 [384, 12], P(('row', 'col'), 'layer'), may hold values from 0 to 511, as said below
- b_blocks: float32 [128, 4, 16, 128, 128], P('row', 'layer', 'col'), may hold values from -6 to 6
- b_cols: int32 [128, 4, 16], P('row', 'layer', 'col'), may hold values from 0 to 511, as said below
- c_cols: int32 [384, 16], P('row', 'col'), may hold values from 0 to 511, as said below
Outputs:
- c_blocks: float32 [384, 16, 128, 128], P(('row', 'layer'), 'col')
The draws below stay inside these ranges and needn't reach their ends.
Inputs may be any that keep to these rules, and one draw needn't show every extreme that they name: a_inner[i, a] % 4 equals a // 3; the inner indices of one row are distinct. b_cols[r, l, t] % 16 equals t; the block columns of one row of B are distinct. c_cols[i, u] % 16 equals u; the kept block columns of one row are distinct.
All inputs are finite; a program needn't handle non-finite values.
Results may differ from the reference program's by a relative error of at most 0.0003.
Values sent between devices are 32-bit elements; how exact they have to be, the bound alone decides.
No kernel may reach another device: no remote copies, remote signals or barrier semaphores. Data moves between devices by JAX's collectives and lax.ppermute only.
A program may use at most 128 MiB of HBM per device.

```python
import jax
import jax.numpy as jnp
from jax import lax

BS = 128
KA = 12
KB = 16
KC = 16
INNER_CLASSES = 4
COL_CLASSES = 16
KAL = 3
BPG = 1
CPG = 1
NR = 384
NWL = 128
NW = 512


def layouts(key):
    key_rows, key_inner, key_cols = jax.random.split(key, 3)
    row_places = jax.random.permutation(key_rows, NR).astype(jnp.int32)
    inner_order = jax.random.permutation(key_inner, NWL).astype(jnp.int32)
    col_order = jax.random.permutation(key_cols, NW // COL_CLASSES).astype(jnp.int32)
    return (row_places, inner_order, col_order)


def draw_a_inner(key, part):
    row_places, inner_order, col_order = layouts(key)
    key = jax.random.fold_in(key, 3)
    shifts = jax.random.randint(key, (NR, INNER_CLASSES), 0, 2).astype(jnp.int32)
    slot_ids = jnp.arange(KA, dtype=jnp.int32)
    slot_class = slot_ids // KAL
    slot_step = slot_ids % KAL
    places = row_places * NW // NR
    quotient = (places[:, None] // INNER_CLASSES + slot_step[None, :] - 1 + shifts[:, slot_class]) % NWL
    return inner_order[quotient] * INNER_CLASSES + slot_class[None, :]


def draw_b_cols(key, part):
    row_places, inner_order, col_order = layouts(key)
    key = jax.random.fold_in(key, 5)
    ranks = jnp.zeros((NWL,), jnp.int32).at[inner_order].set(jnp.arange(NWL, dtype=jnp.int32))
    places = ranks[:, None] * INNER_CLASSES + jnp.arange(INNER_CLASSES, dtype=jnp.int32)[None, :]
    shifts = jax.random.randint(key, (NWL, INNER_CLASSES, COL_CLASSES), 0, 3).astype(jnp.int32)
    slot_ids = jnp.arange(KB, dtype=jnp.int32)
    slot_class = slot_ids // BPG
    slot_step = slot_ids % BPG
    bins = (places[:, :, None] // COL_CLASSES + slot_step[None, None, :] + shifts[:, :, slot_class]) % (NW // COL_CLASSES)
    return col_order[bins] * COL_CLASSES + slot_class[None, None, :]


def draw_c_cols(key, part):
    row_places, inner_order, col_order = layouts(key)
    key = jax.random.fold_in(key, 7)
    shifts = jax.random.randint(key, (NR, COL_CLASSES), 0, 3).astype(jnp.int32)
    slot_ids = jnp.arange(KC, dtype=jnp.int32)
    slot_class = slot_ids // CPG
    slot_step = slot_ids % CPG
    places = row_places * NW // NR
    bins = (places[:, None] // COL_CLASSES + slot_step[None, :] + shifts[:, slot_class]) % (NW // COL_CLASSES)
    return col_order[bins] * COL_CLASSES + slot_class[None, :]


def shard_levels(rng, dims, cuts, low, top_value):
    level, own = 1.0, jax.random.fold_in(rng, 6)
    for dim, parts in cuts:
        steps = jnp.exp(jax.random.uniform(jax.random.fold_in(own, dim), (parts,), jnp.float32, low / len(cuts), top_value / len(cuts)))
        level = level * jnp.repeat(steps, dims[dim] // parts).reshape([-1 if axis == dim else 1 for axis in range(len(dims))])
    return level


def bell_draw(key, dims, scale, most, pieces=(), kind=jnp.bfloat16):
    values = jax.random.normal(key, dims, jnp.float32) * scale
    if len(pieces) > 0:
        values = shard_levels(key, dims, pieces, -0.22, 0.18) * values
    return jnp.clip(values, min=-most, max=most).astype(kind)


def setup_inputs(seed: int = 0) -> dict:
    key_list = jax.random.split(jax.random.key(seed), 6)
    a_blocks = bell_draw(key_list[0], (NR, KA, BS, BS), BS ** -0.5, 0.5, ((0, 64), (1, 4)), jnp.float32)
    a_inner = draw_a_inner(jax.random.fold_in(key_list[5], 71), 0)
    b_blocks = bell_draw(key_list[2], (NWL, INNER_CLASSES, KB, BS, BS), 1.0, 6.0, ((0, 4), (1, 4), (2, 16)), jnp.float32)
    b_cols = draw_b_cols(jax.random.fold_in(key_list[5], 71), 0)
    c_cols = draw_c_cols(jax.random.fold_in(key_list[5], 71), 0)
    return {"a_blocks": a_blocks, "a_inner": a_inner, "b_blocks": b_blocks, "b_cols": b_cols, "c_cols": c_cols}


def reference(a_blocks, a_inner, b_blocks, b_cols, c_cols):
    b_by_inner = b_blocks.reshape(NW, KB, BS, BS)
    b_col_ids = b_cols.reshape(NW, KB)

    def row_product(row_data):
        blocks, inner_ids, kept_cols = row_data
        b_picked = b_by_inner[inner_ids]
        matches = (b_col_ids[inner_ids][:, :, None] == kept_cols[None, None, :]).astype(jnp.float32)
        products = jnp.einsum("axy,atyz->atxz", blocks, b_picked, precision=lax.Precision.HIGHEST)
        return jnp.einsum("atc,atxz->cxz", matches, products, precision=lax.Precision.HIGHEST)

    return lax.map(row_product, (a_blocks, a_inner, c_cols))
```

```python
import functools

import jax
import jax.numpy as jnp
from jax import lax
from jax.experimental import pallas as pl
from jax.experimental.pallas import tpu as pltpu
from jax.sharding import Mesh, PartitionSpec as P

BS = 128
ROWS = 6
KAL = 3
NB = 32
IDX = 256
OFF_B = ROWS * KAL
OFF_C = OFF_B + NB
PASSES = ((0, 6),)


def shift(value, axes, size, step):
    return lax.ppermute(value, axes, [(i, (i + step) % size) for i in range(size)])


def shift_x(value, step):
    at = lambda x: (x % 2) * 2 + x % 4 // 2
    return lax.ppermute(value, ("xl", "xh"), [(at(x), at(x + step)) for x in range(4)])


def device_index(xl, co, z, xh):
    return (((xl * 2 + co) * 8 + z) * 2 + xh) * IDX


def split(value):
    high = value.astype(jnp.bfloat16)
    low = (value - high.astype(jnp.float32)).astype(jnp.bfloat16)
    return high, low


def product_kernel(first, rows, n_a, n_b, place, table, *refs):
    a_refs, refs = refs[:n_a], refs[n_a:]
    b_refs, refs = refs[:n_b], refs[n_b:]
    outs, (a_v, b_v, c_v, a_sem, b_sem, c_sem) = refs[:8], refs[8:]
    xl, co, z, xh, y = (place[i] for i in range(5))
    x = xh * 2 + xl
    n = rows * KAL

    copies = []
    for i, ref in enumerate(a_refs[:7]):
        step = (0, 7, 1, 6, 2, 5, 3)[i]
        copies.append(pltpu.make_async_copy(ref, a_v.at[pl.ds(step * n, n)], a_sem))
    half = n // 2
    copies.append(pltpu.make_async_copy(a_refs[7], a_v.at[pl.ds(4 * n, half)], a_sem))
    copies.append(pltpu.make_async_copy(a_refs[8], a_v.at[pl.ds(4 * n + half, n - half)], a_sem))
    for i, ref in enumerate(b_refs):
        step, lead, count = ((0, 0, NB), (3, 0, NB), (1, 0, NB), (2, 0, NB // 2), (2, NB // 2, NB // 2))[i // 2]
        there = lax.rem(x + step, 4)
        core = co if i % 2 == 0 else 1 - co
        slot = jnp.where(there // 2 == xh, 0, 1)
        start = slot * 4 * NB + (lax.rem(there, 2) * 2 + core) * NB + lead
        copies.append(pltpu.make_async_copy(ref, b_v.at[pl.ds(start, count)], b_sem))
    for copy in copies:
        copy.start()
    for copy in copies:
        copy.wait()

    def one_row(d, h, i):
        there = 2 * lax.rem(y + d, 4) + h
        chunk = lax.rem(there - z + 8, 8)
        row = first + i
        a_at = device_index(xl, co, there, xh) + row * KAL
        c_at = OFF_C + (there * 2 + xh) * ROWS + row
        kept = (table[device_index(xl, co, z, xh) + c_at], table[device_index(xl, co, z, 1 - xh) + c_at])
        total = [jnp.zeros((BS, BS), jnp.float32)] * 2
        for a in range(KAL):
            k = table[a_at + a] // 4
            owner, j = k // NB, lax.rem(k, NB)
            block_high, block_low = split(a_v[chunk * n + i * KAL + a])
            picked = jnp.concatenate((b_v[k], b_v[4 * NB + k]), axis=1)
            picked_high, picked_low = split(picked)
            dot = functools.partial(jnp.dot, preferred_element_type=jnp.float32)
            product = dot(block_high, picked_high) + (dot(block_low, picked_high) + dot(block_high, picked_low))
            for s in range(2):
                col = table[device_index(owner // 2, lax.rem(owner, 2), z, xh if s == 0 else 1 - xh) + OFF_B + j]
                match = jnp.where(col == kept[s], 1.0, 0.0).astype(jnp.float32)
                total[s] = total[s] + match * product[:, s * BS:(s + 1) * BS]
        for s in range(2):
            c_v[d * 2 + h, s, i] = total[s]

    done = []
    for d in (2, 1, 3, 0):
        for h in range(2):
            def body(i, carry, d=d, h=h):
                one_row(d, h, i)
                return carry

            lax.fori_loop(0, rows, body, 0)
            done.append(pltpu.make_async_copy(c_v.at[d * 2 + h], outs[d * 2 + h], c_sem))
            done[-1].start()
    for copy in done:
        copy.wait()


def products(first, rows, place, table, a_parts, b_parts):
    n = rows * KAL
    out = jax.ShapeDtypeStruct((2, rows, BS, BS), jnp.float32)
    anywhere = pl.BlockSpec(memory_space=pl.ANY)
    scalars = pl.BlockSpec(memory_space=pltpu.SMEM)
    return pl.pallas_call(
        functools.partial(product_kernel, first, rows, len(a_parts), len(b_parts)),
        out_shape=[out] * 8,
        in_specs=[scalars, scalars] + [anywhere] * (len(a_parts) + len(b_parts)),
        out_specs=[anywhere] * 8,
        scratch_shapes=[
            pltpu.VMEM((8 * n, BS, BS), jnp.float32),
            pltpu.VMEM((8 * NB, BS, BS), jnp.float32),
            pltpu.VMEM((8, 2, rows, BS, BS), jnp.float32),
            pltpu.SemaphoreType.DMA,
            pltpu.SemaphoreType.DMA,
            pltpu.SemaphoreType.DMA,
        ],
        compiler_params=pltpu.CompilerParams(vmem_limit_bytes=48 * 1024 * 1024),
    )(place, table, *a_parts, *b_parts)


def gather_a(blocks):
    n = blocks.shape[0]
    right = left = blocks
    parts = [blocks]
    for _ in range(3):
        right, left = shift(right, "z", 8, 1), shift(left, "z", 8, -1)
        parts += [right, left]
    parts += [shift(right[:n // 2], "z", 8, 1), shift(left[n // 2:], "z", 8, -1)]
    return parts


def gather_b(blocks):
    parts = [blocks, shift(blocks, "co", 2, 1)]
    right, left = shift_x(blocks, 1), shift_x(blocks, -1)
    far = (shift_x(right[:NB // 2], 1), shift_x(left[NB // 2:], -1))
    for part in (right, left) + far:
        parts += [part, shift(part, "co", 2, 1)]
    return parts


def scatter_sum(outs):
    far_right = shift(outs[4], "y", 4, 1)
    far_left = shift(outs[5], "y", 4, -1)
    right = (shift(outs[2] + far_right, "y", 4, 1), shift(outs[3], "y", 4, 1))
    left = (shift(outs[6], "y", 4, -1), shift(outs[7] + far_left, "y", 4, -1))
    sums = [outs[h] + right[h] + left[h] for h in range(2)]
    mine = jnp.stack([s[0] for s in sums])
    other = shift(jnp.stack([s[1] for s in sums]), "xh", 2, 1)
    return mine, other


def per_device(a_blocks, a_inner, b_blocks, b_cols, c_cols):
    place = jnp.stack([lax.axis_index(name) for name in ("xl", "co", "z", "xh", "y")])
    ids = jnp.concatenate([a_inner.reshape(-1), b_cols.reshape(-1), c_cols.reshape(-1)])
    ids = jnp.pad(ids, (0, IDX - ids.shape[0]))
    table = lax.all_gather(ids, ("xl", "co", "z", "xh"), axis=0, tiled=True)
    b_parts = gather_b(b_blocks.reshape(NB, BS, BS))
    mine, other = [], []
    for first, rows in PASSES:
        a_parts = gather_a(a_blocks[first:first + rows].reshape(rows * KAL, BS, BS))
        outs = products(first, rows, place, table, a_parts, b_parts)
        own_part, other_part = scatter_sum(outs)
        mine.append(own_part)
        other.append(other_part)
    mine, other = jnp.concatenate(mine, axis=1), jnp.concatenate(other, axis=1)
    xh = lax.axis_index("xh")
    result = jnp.stack([jnp.where(xh == 0, mine, other), jnp.where(xh == 0, other, mine)], axis=1)
    return result.reshape(4 * ROWS, 1, BS, BS)


def solution(mesh):
    fine = Mesh(mesh.devices.reshape(2, 2, 8, 2, 4), ("xl", "co", "z", "xh", "y"))
    return jax.shard_map(
        per_device,
        mesh=fine,
        in_specs=(
            P(("xl", "co", "z", "xh"), "y", None, None),
            P(("xl", "co", "z", "xh"), "y"),
            P(("xl", "co"), "y", ("z", "xh"), None, None),
            P(("xl", "co"), "y", ("z", "xh")),
            P(("xl", "co"), ("z", "xh")),
        ),
        out_specs=P(("xl", "co", "y"), ("z", "xh"), None, None),
        check_vma=False,
    )
```

```python
import functools

import jax
import jax.numpy as jnp
from jax import lax
from jax.experimental import pallas as pl
from jax.experimental.pallas import tpu as pltpu
from jax.sharding import Mesh, PartitionSpec as P

BS = 128
ROWS = 6
KAL = 3
NB = 32
TILE = 8
def shift(value, axis, size, step):
    return lax.ppermute(value, axis, [(i, (i + step) % size) for i in range(size)])


def split(value):
    high = value.astype(jnp.bfloat16)
    low = (value - high.astype(jnp.float32)).astype(jnp.bfloat16)
    return high, low


def with_ids(blocks, *ids):
    tile = jnp.stack([jnp.pad(row.reshape(-1), (0, BS - row.size)) for row in ids])
    tile = jnp.pad(tile.astype(jnp.float32), ((0, TILE - len(ids)), (0, 0)))
    return jnp.concatenate([blocks.reshape(-1, BS), tile])


def product_kernel(spans, n_b, place, *refs):
    a_refs, refs = refs[:len(spans)], refs[len(spans):]
    b_refs, refs = refs[:n_b], refs[n_b:]
    outs, (a_v, b_v, c_v, ids_f, ids_v, table, sems) = refs[:8], refs[8:]
    xl, co, z, xh, y = (place[i] for i in range(5))
    x = xh * 2 + xl

    chunks = []
    for (step, low, high), ref in zip(spans, a_refs):
        if step not in chunks:
            chunks.append(step)
    ids, copies = [], []
    for (step, low, high), ref in zip(spans, a_refs):
        at, count = chunks.index(step) * ROWS * KAL * BS + low * KAL * BS, (high - low) * KAL * BS
        copies.append(pltpu.make_async_copy(ref.at[pl.ds(0, count)], a_v.at[pl.ds(at, count)], sems.at[11]))
        if high == ROWS:
            at = chunks.index(step) * TILE
            ids.append(pltpu.make_async_copy(ref.at[pl.ds(count, TILE)], ids_f.at[pl.ds(at, TILE)], sems.at[1]))
    back = 3 - 2 * co
    for ref, (step, core) in zip(b_refs, ((0, 0), (0, 1), (back, 0), (back, 1), (2, 0), (4 - back, 1), (4 - back, 0), (2, 1))):
        there = lax.rem(x + step, 4)
        core = lax.rem(co + core, 2)
        slot = jnp.where(there // 2 == xh, 0, 1)
        owner = slot * 4 + lax.rem(there, 2) * 2 + core
        at = pl.multiple_of(owner * NB * BS, BS)
        copies.append(pltpu.make_async_copy(ref.at[pl.ds(0, NB * BS)], b_v.at[pl.ds(at, NB * BS)], sems.at[0]))
        at = pl.multiple_of((4 + owner) * TILE, TILE)
        ids.append(pltpu.make_async_copy(ref.at[pl.ds(NB * BS, TILE)], ids_f.at[pl.ds(at, TILE)], sems.at[1]))
    for copy in ids + copies:
        copy.start()
    for copy in ids:
        copy.wait()
    ids_v[...] = ids_f[...].astype(jnp.int32)
    to_table = pltpu.make_async_copy(ids_v, table, sems.at[2])
    to_table.start()
    for copy in copies:
        copy.wait()
    to_table.wait()

    def block(ref, i):
        return ref[pl.ds(pl.multiple_of(i * BS, BS), BS), :]

    def one_row(step, ref, at, i):
        chunk = chunks.index(step)
        there = lax.rem(z + step, 8)
        c_at = (there * 2 + xh) * ROWS + i
        mine = 4 + xl * 2 + co
        kept = (table[mine * TILE + 1, c_at], table[(mine + 4) * TILE + 1, c_at])
        total = [jnp.zeros((BS, BS), jnp.float32)] * 2
        for a in range(KAL):
            k = table[chunk * TILE, i * KAL + a] // 4
            a_high, a_low = split(block(ref, at + a))
            b_high, b_low = split(jnp.concatenate((block(b_v, k), block(b_v, 4 * NB + k)), axis=1))
            product = jnp.dot(
                jnp.concatenate((a_high, a_low, a_high), axis=1),
                jnp.concatenate((b_high, b_high, b_low), axis=0),
                preferred_element_type=jnp.float32,
            )
            owner, j = k // NB, lax.rem(k, NB)
            for s in range(2):
                col = table[(4 + s * 4 + owner) * TILE, j]
                match = jnp.where(col == kept[s], 1.0, 0.0).astype(jnp.float32)
                total[s] = total[s] + match * product[:, s * BS:(s + 1) * BS]
        for s in range(2):
            c_v[chunk, s, i] = total[s]

    for (step, low, high), ref in zip(spans, a_refs):
        for i in range(low, high):
            one_row(step, a_v, (chunks.index(step) * ROWS + i) * KAL, i)
        if high == ROWS:
            layer = lax.rem(lax.rem(z + step, 8) // 2 - y + 4, 4)
            for d in range(4):
                @pl.when(layer == d)
                def _(d=d, chunk=chunks.index(step)):
                    for s in range(2):
                        pltpu.make_async_copy(c_v.at[chunk, s], outs[d * 2 + s], sems.at[3 + d * 2 + s]).start()
    for i in range(8):
        pltpu.make_async_copy(c_v.at[i // 2, i % 2], outs[i], sems.at[3 + i]).wait()


def products(place, spans, a_parts, b_parts):
    n = ROWS * KAL
    out = jax.ShapeDtypeStruct((ROWS, BS, BS), jnp.float32)
    anywhere = pl.BlockSpec(memory_space=pl.ANY)
    far_memory = pl.BlockSpec(memory_space=pl.ANY)
    return pl.pallas_call(
        functools.partial(product_kernel, spans, len(b_parts)),
        out_shape=[out] * 8,
        in_specs=[pl.BlockSpec(memory_space=pltpu.SMEM)]
        + [far_memory] * len(a_parts)
        + [far_memory] * len(b_parts),
        out_specs=[anywhere] * 8,
        scratch_shapes=[
            pltpu.VMEM((4 * n * BS, BS), jnp.float32),
            pltpu.VMEM((8 * NB * BS, BS), jnp.float32),
            pltpu.VMEM((4, 2, ROWS, BS, BS), jnp.float32),
            pltpu.VMEM((12 * TILE, BS), jnp.float32),
            pltpu.VMEM((12 * TILE, BS), jnp.int32),
            pltpu.SMEM((12 * TILE, BS), jnp.int32),
            pltpu.SemaphoreType.DMA((12,)),
        ],
        compiler_params=pltpu.CompilerParams(vmem_limit_bytes=48 * 1024 * 1024),
        cost_estimate=pl.CostEstimate(
            flops=8 * n * BS ** 3 * 6, bytes_accessed=(4 * n + 8 * NB + 8 * ROWS) * BS * BS * 4, transcendentals=0
        ),
    )(place, *a_parts, *b_parts)


def swap(value):
    return shift(value, "co", 2, 1)


def pass_on(value):
    at = lambda x, core: (x % 2) * 4 + core * 2 + x % 4 // 2
    pairs = [(at(x, core), at(x + 1 - 2 * core, core)) for x in range(4) for core in range(2)]
    return lax.ppermute(value, ("xl", "co", "xh"), pairs)


def ring_step(right, left):
    return shift(right, "z", 8, 1), shift(left, "z", 8, -1)


def gather(a, b):
    r1, l1, near, other = together(*ring_step(a, a), pass_on(b), swap(b))
    r2, l2, near_other, near_swap = together(*ring_step(r1, l1), pass_on(other), swap(near))
    r3, l3, far, near_other_swap = together(*ring_step(r2, l2), pass_on(near), swap(near_other))
    half = ROWS // 2 * KAL * BS
    r4, l4 = ring_step(r3[:half], l3[half:])
    b_parts = [b, other, near, near_other, far, near_swap, near_other_swap, swap(far)]
    return (r1, l1, r3, l3), (a, r2, l2, r4, l4), b_parts


def together(*values):
    return lax.optimization_barrier(values)


def up(value):
    return shift(value, "y", 4, 1)


def down(value):
    return shift(value, "y", 4, -1)


def per_device(a_blocks, a_inner, b_blocks, b_cols, c_cols):
    place = jnp.stack([lax.axis_index(name) for name in ("xl", "co", "z", "xh", "y")])
    odd, even, b_parts = gather(with_ids(a_blocks, a_inner), with_ids(b_blocks, b_cols, c_cols))
    p = products(place, ((7, 0, 6), (1, 0, 6), (5, 0, 6), (3, 0, 6)), odd, b_parts)
    p_far = up(p[4]), down(p[5])
    p_plain = up(p[3]), down(p[6])
    q = products(place, ((0, 0, 6), (6, 0, 6), (2, 0, 6), (4, 0, 3), (4, 3, 6)), even, b_parts)
    p2, p7, p_far, p_plain, _ = together(p[2], p[7], p_far, p_plain, q[0])
    q_far = up(q[4]), down(q[5])
    p_near = up(p2 + p_far[0]), down(p7 + p_far[1])
    q2, q3, q6, q7, q_far, p_near = together(q[2], q[3], q[6], q[7], q_far, p_near)
    p_other = shift(p[1] + p_plain[0] + p_near[1], "xh", 2, 1)
    p_mine = p[0] + p_near[0] + p_plain[1]
    q_near = up(q2 + q_far[0]), down(q7 + q_far[1])
    q_plain = up(q3), down(q6)
    q_mine = q[0] + q_near[0] + q_plain[1]
    q_other = shift(q[1] + q_plain[0] + q_near[1], "xh", 2, 1)
    own_parity = lax.axis_index("z") % 2
    own_half = lax.axis_index("xh")
    rows = []
    for parity in range(2):
        mine = jnp.where(own_parity == parity, q_mine, p_mine)
        other = jnp.where(own_parity == parity, q_other, p_other)
        rows += [jnp.where(own_half == 0, mine, other), jnp.where(own_half == 0, other, mine)]
    return jnp.stack(rows).reshape(4 * ROWS, 1, BS, BS)


def solution(mesh):
    fine = Mesh(mesh.devices.reshape(2, 2, 8, 2, 4), ("xl", "co", "z", "xh", "y"))
    return jax.shard_map(
        per_device,
        mesh=fine,
        in_specs=(
            P(("xl", "co", "z", "xh"), "y", None, None),
            P(("xl", "co", "z", "xh"), "y"),
            P(("xl", "co"), "y", ("z", "xh"), None, None),
            P(("xl", "co"), "y", ("z", "xh")),
            P(("xl", "co"), ("z", "xh")),
        ),
        out_specs=P(("xl", "co", "y"), ("z", "xh"), None, None),
        check_vma=False,
    )
```

```python
import functools

import jax
import jax.numpy as jnp
from jax import lax
from jax.experimental import pallas as pl
from jax.experimental.pallas import tpu as pltpu
from jax.sharding import Mesh, PartitionSpec as P

BS = 128
ROWS = 6
KAL = 3
NB = 32
TILE = 8
PAIRED = {(2, 0): (0, 0), (1, 1): (0, ROWS), (2, 1): (1, 0), (3, 0): (1, ROWS), (0, 0): (2, 0), (0, 1): (3, 0), (1, 0): (4, 0), (3, 1): (5, 0)}
SINGLE = {(d, s): (2 * d + s, 0) for d in range(4) for s in range(2)}


def shift(value, axis, size, step):
    return lax.ppermute(value, axis, [(i, (i + step) % size) for i in range(size)])


def split(value):
    high = value.astype(jnp.bfloat16)
    low = (value - high.astype(jnp.float32)).astype(jnp.bfloat16)
    return high, low


def with_ids(blocks, *ids):
    tile = jnp.stack([jnp.pad(row.reshape(-1), (0, BS - row.size)) for row in ids])
    tile = jnp.pad(tile.astype(jnp.float32), ((0, TILE - len(ids)), (0, 0)))
    return jnp.concatenate([blocks.reshape(-1, BS), tile])


def product_kernel(spans, routes, n_b, place, *refs):
    a_refs, refs = refs[:4], refs[4:]
    b_refs, refs = refs[:n_b], refs[n_b:]
    outs, (a_v, b_v, c_v, ids_f, ids_v, table, sems) = refs[:-7], refs[-7:]
    xl, co, z, xh, y = (place[i] for i in range(5))
    x = xh * 2 + xl

    ids, copies, chunks = [], [], []
    size = ROWS * KAL * BS
    for chunk, ref in enumerate(a_refs):
        chunks.append(pltpu.make_async_copy(ref.at[pl.ds(0, size)], a_v.at[pl.ds(chunk * size, size)], sems.at[11 + chunk]))
        ids.append(pltpu.make_async_copy(ref.at[pl.ds(size, TILE)], ids_f.at[pl.ds(chunk * TILE, TILE)], sems.at[1]))
    back = 3 - 2 * co
    for ref, (step, core) in zip(b_refs, ((0, 0), (0, 1), (back, 0), (back, 1), (2, 0), (4 - back, 1), (4 - back, 0), (2, 1))):
        there = lax.rem(x + step, 4)
        core = lax.rem(co + core, 2)
        slot = jnp.where(there // 2 == xh, 0, 1)
        owner = slot * 4 + lax.rem(there, 2) * 2 + core
        at = pl.multiple_of(owner * NB * BS, BS)
        copies.append(pltpu.make_async_copy(ref.at[pl.ds(0, NB * BS)], b_v.at[pl.ds(at, NB * BS)], sems.at[0]))
        at = pl.multiple_of((4 + owner) * TILE, TILE)
        ids.append(pltpu.make_async_copy(ref.at[pl.ds(NB * BS, TILE)], ids_f.at[pl.ds(at, TILE)], sems.at[1]))
    for copy in ids + copies + chunks:
        copy.start()
    for copy in ids:
        copy.wait()
    ids_v[...] = ids_f[...].astype(jnp.int32)
    to_table = pltpu.make_async_copy(ids_v, table, sems.at[2])
    to_table.start()
    for copy in copies:
        copy.wait()
    to_table.wait()

    def block(ref, i):
        return ref[pl.ds(pl.multiple_of(i * BS, BS), BS), :]

    def one_row(chunk, there, i):
        c_at = (there * 2 + xh) * ROWS + i
        mine = 4 + xl * 2 + co
        kept = (table[mine * TILE + 1, c_at], table[(mine + 4) * TILE + 1, c_at])
        total = [jnp.zeros((BS, BS), jnp.float32)] * 2
        for a in range(KAL):
            k = table[chunk * TILE, i * KAL + a] // 4
            a_high, a_low = split(block(a_v, (chunk * ROWS + i) * KAL + a))
            b_high, b_low = split(jnp.concatenate((block(b_v, k), block(b_v, 4 * NB + k)), axis=1))
            product = jnp.dot(
                jnp.concatenate((a_high, a_low, a_high), axis=1),
                jnp.concatenate((b_high, b_high, b_low), axis=0),
                preferred_element_type=jnp.float32,
            )
            owner, j = k // NB, lax.rem(k, NB)
            for s in range(2):
                col = table[(4 + s * 4 + owner) * TILE, j]
                match = jnp.where(col == kept[s], 1.0, 0.0).astype(jnp.float32)
                total[s] = total[s] + match * product[:, s * BS:(s + 1) * BS]
        for s in range(2):
            c_v[chunk, s, i] = total[s]

    def place_of(d, s):
        out, at = routes[d, s]
        return outs[out].at[pl.ds(at, ROWS)]

    for chunk, (distance, kept_core) in enumerate(spans):
        there = lax.rem(z + jnp.where(co == kept_core, 8 - distance, distance), 8)
        chunks[chunk].wait()
        for i in range(ROWS):
            one_row(chunk, there, i)
        layer = lax.rem(there // 2 - y + 4, 4)
        for d in range(4):
            @pl.when(layer == d)
            def _(d=d, chunk=chunk):
                for s in range(2):
                    pltpu.make_async_copy(c_v.at[chunk, s], place_of(d, s), sems.at[3 + d * 2 + s]).start()
    for i in range(8):
        pltpu.make_async_copy(c_v.at[i // 2, i % 2], place_of(i // 2, i % 2), sems.at[3 + i]).wait()


def products(place, spans, routes, a_parts, b_parts):
    n = ROWS * KAL
    places = list(routes.values())
    out_rows = [ROWS + max(at for out, at in places if out == i) for i in range(1 + max(places)[0])]
    anywhere = pl.BlockSpec(memory_space=pl.ANY)
    far_memory = pl.BlockSpec(memory_space=pl.ANY)
    return pl.pallas_call(
        functools.partial(product_kernel, spans, routes, len(b_parts)),
        out_shape=[jax.ShapeDtypeStruct((rows, BS, BS), jnp.float32) for rows in out_rows],
        in_specs=[pl.BlockSpec(memory_space=pltpu.SMEM)]
        + [far_memory] * len(a_parts)
        + [far_memory] * len(b_parts),
        out_specs=[anywhere] * len(out_rows),
        scratch_shapes=[
            pltpu.VMEM((4 * n * BS, BS), jnp.float32),
            pltpu.VMEM((8 * NB * BS, BS), jnp.float32),
            pltpu.VMEM((4, 2, ROWS, BS, BS), jnp.float32),
            pltpu.VMEM((12 * TILE, BS), jnp.float32),
            pltpu.VMEM((12 * TILE, BS), jnp.int32),
            pltpu.SMEM((12 * TILE, BS), jnp.int32),
            pltpu.SemaphoreType.DMA((15,)),
        ],
        compiler_params=pltpu.CompilerParams(vmem_limit_bytes=58 * 1024 * 1024),
        cost_estimate=pl.CostEstimate(
            flops=8 * n * BS ** 3 * 6, bytes_accessed=(4 * n + 8 * NB + 8 * ROWS) * BS * BS * 4, transcendentals=0
        ),
    )(place, *a_parts, *b_parts)


def swap(value):
    return shift(value, "co", 2, 1)


def pass_on(value):
    at = lambda x, core: (x % 2) * 4 + core * 2 + x % 4 // 2
    pairs = [(at(x, core), at(x + 1 - 2 * core, core)) for x in range(4) for core in range(2)]
    return lax.ppermute(value, ("xl", "co", "xh"), pairs)


def pass_z(value):
    pairs = [(core * 8 + z, core * 8 + (z + 1 - 2 * core) % 8) for z in range(8) for core in range(2)]
    return lax.ppermute(value, ("co", "z"), pairs)


def gather(a, b):
    own, other = [a], [swap(a)]
    for _ in range(2):
        own.append(pass_z(own[-1]))
        other.append(pass_z(other[-1]))
    b_other = swap(b)
    near, near_other, own[2], other[2] = together(pass_on(b), pass_on(b_other), own[2], other[2])
    far = pass_on(near)
    own.append(pass_z(own[2]))
    other.append(pass_z(other[2]))
    last = pass_z(own[3])
    near, near_other, own[3] = together(near, near_other, own[3])
    far, own[3] = together(far, own[3])
    odd = (own[1], swap(other[1]), own[3], swap(other[3]))
    even = (a, own[2], swap(other[2]), last)
    return odd, even, [b, b_other, near, near_other, far, swap(near), swap(near_other), swap(far)]


def together(*values):
    return lax.optimization_barrier(values)


def up(value):
    return shift(value, "y", 4, 1)


def down(value):
    return shift(value, "y", 4, -1)


def per_device(a_blocks, a_inner, b_blocks, b_cols, c_cols):
    place = jnp.stack([lax.axis_index(name) for name in ("xl", "co", "z", "xh", "y")])
    odd, even, b_parts = gather(with_ids(a_blocks, a_inner), with_ids(b_blocks, b_cols, c_cols))
    p = products(place, ((1, 0), (1, 1), (3, 0), (3, 1)), PAIRED, odd, b_parts)
    p_up, p_down, p_0, p_1, p_near_0, p_near_1 = p
    p_up, p_down = up(p_up), down(p_down)
    q = products(place, ((0, 0), (2, 0), (2, 1), (4, 0)), SINGLE, even, b_parts)
    p_up, p_down, _ = together(p_up, p_down, q[0])
    p_near_0, p_near_1 = up(p_near_0 + p_up[:ROWS]), down(p_near_1 + p_down[:ROWS])
    q_far_1, q_plain_1, q_far_0 = down(q[5]), up(q[3]), up(q[4])
    q7, q6, q_far_1, p_near_0, p_near_1 = together(q[7], q[6], q_far_1, p_near_0, p_near_1)
    p_other = shift(p_1 + p_up[ROWS:] + p_near_1, "xh", 2, 1)
    p_mine = p_0 + p_near_0 + p_down[ROWS:]
    q_near_1, q_plain_0 = down(q7 + q_far_1), down(q6)
    q_other = shift(q[1] + q_plain_1 + q_near_1, "xh", 2, 1)
    q_near_0 = up(q[2] + q_far_0)
    q_mine = q[0] + q_near_0 + q_plain_0
    own_parity = lax.axis_index("z") % 2
    own_half = lax.axis_index("xh")
    rows = []
    for parity in range(2):
        mine = jnp.where(own_parity == parity, q_mine, p_mine)
        other = jnp.where(own_parity == parity, q_other, p_other)
        rows += [jnp.where(own_half == 0, mine, other), jnp.where(own_half == 0, other, mine)]
    return jnp.stack(rows).reshape(4 * ROWS, 1, BS, BS)


def solution(mesh):
    fine = Mesh(mesh.devices.reshape(2, 2, 8, 2, 4), ("xl", "co", "z", "xh", "y"))
    return jax.shard_map(
        per_device,
        mesh=fine,
        in_specs=(
            P(("xl", "co", "z", "xh"), "y", None, None),
            P(("xl", "co", "z", "xh"), "y"),
            P(("xl", "co"), "y", ("z", "xh"), None, None),
            P(("xl", "co"), "y", ("z", "xh")),
            P(("xl", "co"), ("z", "xh")),
        ),
        out_specs=P(("xl", "co", "y"), ("z", "xh"), None, None),
        check_vma=False,
    )
```

```python
import functools

import jax
import jax.numpy as jnp
from jax import lax
from jax.experimental import pallas as pl
from jax.experimental.pallas import tpu as pltpu
from jax.sharding import Mesh, PartitionSpec as P

BS = 128
ROWS = 6
KAL = 3
NB = 32
TILE = 8
PAIRED = {(2, 0): (0, 0), (1, 1): (0, ROWS), (2, 1): (1, 0), (3, 0): (1, ROWS), (0, 0): (2, 0), (0, 1): (3, 0), (1, 0): (4, 0), (3, 1): (5, 0)}
SINGLE = {(d, s): (2 * d + s, 0) for d in range(4) for s in range(2)}


def shift(value, axis, size, step):
    return lax.ppermute(value, axis, [(i, (i + step) % size) for i in range(size)])


def split(value):
    high = value.astype(jnp.bfloat16)
    low = (value - high.astype(jnp.float32)).astype(jnp.bfloat16)
    return high, low


def with_ids(blocks, *ids):
    tile = jnp.stack([jnp.pad(row.reshape(-1), (0, BS - row.size)) for row in ids])
    tile = jnp.pad(tile.astype(jnp.float32), ((0, TILE - len(ids)), (0, 0)))
    return jnp.concatenate([blocks.reshape(-1, BS), tile])


def product_kernel(spans, routes, n_b, place, *refs):
    a_refs, refs = refs[:4], refs[4:]
    b_refs, refs = refs[:n_b], refs[n_b:]
    outs, (a_v, b_v, c_v, ids_f, ids_v, table, sems) = refs[:-7], refs[-7:]
    xl, co, z, xh, y = (place[i] for i in range(5))
    x = xh * 2 + xl

    ids, copies, chunks = [], [], []
    size = ROWS * KAL * BS
    for chunk, ref in enumerate(a_refs):
        chunks.append(pltpu.make_async_copy(ref.at[pl.ds(0, size)], a_v.at[pl.ds(chunk * size, size)], sems.at[11 + chunk]))
        ids.append(pltpu.make_async_copy(ref.at[pl.ds(size, TILE)], ids_f.at[pl.ds(chunk * TILE, TILE)], sems.at[1]))
    back = 3 - 2 * co
    for ref, (step, core) in zip(b_refs, ((0, 0), (0, 1), (back, 0), (back, 1), (2, 0), (4 - back, 1), (4 - back, 0), (2, 1))):
        there = lax.rem(x + step, 4)
        core = lax.rem(co + core, 2)
        slot = jnp.where(there // 2 == xh, 0, 1)
        owner = slot * 4 + lax.rem(there, 2) * 2 + core
        at = pl.multiple_of(owner * NB * BS, BS)
        copies.append(pltpu.make_async_copy(ref.at[pl.ds(0, NB * BS)], b_v.at[pl.ds(at, NB * BS)], sems.at[0]))
        at = pl.multiple_of((4 + owner) * TILE, TILE)
        ids.append(pltpu.make_async_copy(ref.at[pl.ds(NB * BS, TILE)], ids_f.at[pl.ds(at, TILE)], sems.at[1]))
    for copy in ids + copies + chunks:
        copy.start()
    for copy in ids:
        copy.wait()
    ids_v[...] = ids_f[...].astype(jnp.int32)
    to_table = pltpu.make_async_copy(ids_v, table, sems.at[2])
    to_table.start()
    for copy in copies:
        copy.wait()
    to_table.wait()

    def block(ref, i):
        return ref[pl.ds(pl.multiple_of(i * BS, BS), BS), :]

    def one_row(chunk, there, i):
        c_at = (there * 2 + xh) * ROWS + i
        mine = 4 + xl * 2 + co
        kept = (table[mine * TILE + 1, c_at], table[(mine + 4) * TILE + 1, c_at])
        total = [jnp.zeros((BS, BS), jnp.float32)] * 2
        for a in range(KAL):
            k = table[chunk * TILE, i * KAL + a] // 4
            a_high, a_low = split(block(a_v, (chunk * ROWS + i) * KAL + a))
            b_high, b_low = split(jnp.concatenate((block(b_v, k), block(b_v, 4 * NB + k)), axis=1))
            product = jnp.dot(
                jnp.concatenate((a_high, a_low, a_high), axis=1),
                jnp.concatenate((b_high, b_high, b_low), axis=0),
                preferred_element_type=jnp.float32,
            )
            owner, j = k // NB, lax.rem(k, NB)
            for s in range(2):
                col = table[(4 + s * 4 + owner) * TILE, j]
                match = jnp.where(col == kept[s], 1.0, 0.0).astype(jnp.float32)
                total[s] = total[s] + match * product[:, s * BS:(s + 1) * BS]
        for s in range(2):
            c_v[chunk, s, i] = total[s]

    def place_of(d, s):
        out, at = routes[d, s]
        return outs[out].at[pl.ds(at, ROWS)]

    for chunk, (distance, kept_core) in enumerate(spans):
        there = lax.rem(z + jnp.where(co == kept_core, 8 - distance, distance), 8)
        chunks[chunk].wait()
        for i in range(ROWS):
            one_row(chunk, there, i)
        layer = lax.rem(there // 2 - y + 4, 4)
        for d in range(4):
            @pl.when(layer == d)
            def _(d=d, chunk=chunk):
                for s in range(2):
                    pltpu.make_async_copy(c_v.at[chunk, s], place_of(d, s), sems.at[3 + d * 2 + s]).start()
    for i in range(8):
        pltpu.make_async_copy(c_v.at[i // 2, i % 2], place_of(i // 2, i % 2), sems.at[3 + i]).wait()


def products(place, spans, routes, a_parts, b_parts):
    n = ROWS * KAL
    places = list(routes.values())
    out_rows = [ROWS + max(at for out, at in places if out == i) for i in range(1 + max(places)[0])]
    anywhere = pl.BlockSpec(memory_space=pl.ANY)
    far_memory = pl.BlockSpec(memory_space=pl.ANY)
    return pl.pallas_call(
        functools.partial(product_kernel, spans, routes, len(b_parts)),
        out_shape=[jax.ShapeDtypeStruct((rows, BS, BS), jnp.float32) for rows in out_rows],
        in_specs=[pl.BlockSpec(memory_space=pltpu.SMEM)]
        + [far_memory] * len(a_parts)
        + [far_memory] * len(b_parts),
        out_specs=[anywhere] * len(out_rows),
        scratch_shapes=[
            pltpu.VMEM((4 * n * BS, BS), jnp.float32),
            pltpu.VMEM((8 * NB * BS, BS), jnp.float32),
            pltpu.VMEM((4, 2, ROWS, BS, BS), jnp.float32),
            pltpu.VMEM((12 * TILE, BS), jnp.float32),
            pltpu.VMEM((12 * TILE, BS), jnp.int32),
            pltpu.SMEM((12 * TILE, BS), jnp.int32),
            pltpu.SemaphoreType.DMA((15,)),
        ],
        compiler_params=pltpu.CompilerParams(vmem_limit_bytes=58 * 1024 * 1024),
        cost_estimate=pl.CostEstimate(
            flops=8 * n * BS ** 3 * 6, bytes_accessed=(4 * n + 8 * NB + 8 * ROWS) * BS * BS * 4, transcendentals=0
        ),
    )(place, *a_parts, *b_parts)


def swap(value):
    return shift(value, "co", 2, 1)


def pass_on(value):
    at = lambda x, core: (x % 2) * 4 + core * 2 + x % 4 // 2
    pairs = [(at(x, core), at(x + 1 - 2 * core, core)) for x in range(4) for core in range(2)]
    return lax.ppermute(value, ("xl", "co", "xh"), pairs)


def pass_z(value):
    pairs = [(core * 8 + z, core * 8 + (z + 1 - 2 * core) % 8) for z in range(8) for core in range(2)]
    return lax.ppermute(value, ("co", "z"), pairs)


def gather(a, b):
    own, other = [a], [swap(a)]
    for _ in range(2):
        own.append(pass_z(own[-1]))
        other.append(pass_z(other[-1]))
    b_other = swap(b)
    near, near_other, own[2], other[2] = together(pass_on(b), pass_on(b_other), own[2], other[2])
    far = pass_on(near)
    own.append(pass_z(own[2]))
    other.append(pass_z(other[2]))
    last = pass_z(own[3])
    near, near_other, own[3] = together(near, near_other, own[3])
    far, own[3] = together(far, own[3])
    odd = (own[1], swap(other[1]), own[3], swap(other[3]))
    even = (a, own[2], swap(other[2]), last)
    return odd, even, [b, b_other, near, near_other, far, swap(near), swap(near_other), swap(far)]


def together(*values):
    return lax.optimization_barrier(values)


def up(value):
    return shift(value, "y", 4, 1)


def down(value):
    return shift(value, "y", 4, -1)


def per_device(a_blocks, a_inner, b_blocks, b_cols, c_cols):
    place = jnp.stack([lax.axis_index(name) for name in ("xl", "co", "z", "xh", "y")])
    odd, even, b_parts = gather(with_ids(a_blocks, a_inner), with_ids(b_blocks, b_cols, c_cols))
    p = products(place, ((1, 0), (1, 1), (3, 0), (3, 1)), PAIRED, odd, b_parts)
    p_up, p_down, p_0, p_1, p_near_0, p_near_1 = p
    p_up, p_down = up(p_up), down(p_down)
    q = products(place, ((0, 0), (2, 0), (2, 1), (4, 0)), SINGLE, even, b_parts)
    p_up, p_down, _ = together(p_up, p_down, q[0])
    p_near_0, p_near_1 = up(p_near_0 + p_up[:ROWS]), down(p_near_1 + p_down[:ROWS])
    q_far_1, q_plain_1, q_far_0 = down(q[5]), up(q[3]), up(q[4])
    q7, q6, q_far_1 = together(q[7], q[6], q_far_1)
    p_other = shift(p_1 + p_up[ROWS:] + p_near_1, "xh", 2, 1)
    p_mine = p_0 + p_near_0 + p_down[ROWS:]
    q_near_1, q_plain_0 = down(q7 + q_far_1), down(q6)
    q_other = shift(q[1] + q_plain_1 + q_near_1, "xh", 2, 1)
    q_near_0 = up(q[2] + q_far_0)
    q_mine = q[0] + q_near_0 + q_plain_0
    own_parity = lax.axis_index("z") % 2
    own_half = lax.axis_index("xh")
    rows = []
    for parity in range(2):
        mine = jnp.where(own_parity == parity, q_mine, p_mine)
        other = jnp.where(own_parity == parity, q_other, p_other)
        rows += [jnp.where(own_half == 0, mine, other), jnp.where(own_half == 0, other, mine)]
    return jnp.stack(rows).reshape(4 * ROWS, 1, BS, BS)


def solution(mesh):
    fine = Mesh(mesh.devices.reshape(2, 2, 8, 2, 4), ("xl", "co", "z", "xh", "y"))
    return jax.shard_map(
        per_device,
        mesh=fine,
        in_specs=(
            P(("xl", "co", "z", "xh"), "y", None, None),
            P(("xl", "co", "z", "xh"), "y"),
            P(("xl", "co"), "y", ("z", "xh"), None, None),
            P(("xl", "co"), "y", ("z", "xh")),
            P(("xl", "co"), ("z", "xh")),
        ),
        out_specs=P(("xl", "co", "y"), ("z", "xh"), None, None),
        check_vma=False,
    )
```

```python
import functools

import jax
import jax.numpy as jnp
from jax import lax
from jax.experimental import pallas as pl
from jax.experimental.pallas import tpu as pltpu
from jax.sharding import Mesh, PartitionSpec as P

BS = 128
ROWS = 6
KAL = 3
NB = 32
TILE = 8
PAIRED = {(2, 0): (0, 0), (1, 1): (0, ROWS), (2, 1): (1, 0), (3, 0): (1, ROWS), (0, 0): (2, 0), (0, 1): (3, 0), (1, 0): (4, 0), (3, 1): (5, 0)}
SINGLE = {(d, s): (2 * d + s, 0) for d in range(4) for s in range(2)}


def shift(value, axis, size, step):
    return lax.ppermute(value, axis, [(i, (i + step) % size) for i in range(size)])


def split(value):
    high = value.astype(jnp.bfloat16)
    low = (value - high.astype(jnp.float32)).astype(jnp.bfloat16)
    return high, low


def with_ids(blocks, *ids):
    tile = jnp.stack([jnp.pad(row.reshape(-1), (0, BS - row.size)) for row in ids])
    tile = jnp.pad(tile.astype(jnp.float32), ((0, TILE - len(ids)), (0, 0)))
    return jnp.concatenate([blocks.reshape(-1, BS), tile])


def product_kernel(spans, routes, n_b, place, *refs):
    a_refs, refs = refs[:4], refs[4:]
    b_refs, refs = refs[:n_b], refs[n_b:]
    outs, (a_v, b_v, c_v, ids_f, ids_v, table, sems) = refs[:-7], refs[-7:]
    xl, co, z, xh, y = (place[i] for i in range(5))
    x = xh * 2 + xl

    ids, copies, chunks = [], [], []
    size = ROWS * KAL * BS
    for chunk, ref in enumerate(a_refs):
        chunks.append(pltpu.make_async_copy(ref.at[pl.ds(0, size)], a_v.at[pl.ds(chunk * size, size)], sems.at[11 + chunk]))
        ids.append(pltpu.make_async_copy(ref.at[pl.ds(size, TILE)], ids_f.at[pl.ds(chunk * TILE, TILE)], sems.at[1]))
    back = 3 - 2 * co
    for ref, (step, core) in zip(b_refs, ((0, 0), (0, 1), (back, 0), (back, 1), (2, 0), (4 - back, 1), (4 - back, 0), (2, 1))):
        there = lax.rem(x + step, 4)
        core = lax.rem(co + core, 2)
        slot = jnp.where(there // 2 == xh, 0, 1)
        owner = slot * 4 + lax.rem(there, 2) * 2 + core
        at = pl.multiple_of(owner * NB * BS, BS)
        copies.append(pltpu.make_async_copy(ref.at[pl.ds(0, NB * BS)], b_v.at[pl.ds(at, NB * BS)], sems.at[0]))
        at = pl.multiple_of((4 + owner) * TILE, TILE)
        ids.append(pltpu.make_async_copy(ref.at[pl.ds(NB * BS, TILE)], ids_f.at[pl.ds(at, TILE)], sems.at[1]))
    for copy in ids + copies + chunks:
        copy.start()
    for copy in ids:
        copy.wait()
    ids_v[...] = ids_f[...].astype(jnp.int32)
    to_table = pltpu.make_async_copy(ids_v, table, sems.at[2])
    to_table.start()
    for copy in copies:
        copy.wait()
    to_table.wait()

    def block(ref, i):
        return ref[pl.ds(pl.multiple_of(i * BS, BS), BS), :]

    def one_row(chunk, there, i):
        c_at = (there * 2 + xh) * ROWS + i
        mine = 4 + xl * 2 + co
        kept = (table[mine * TILE + 1, c_at], table[(mine + 4) * TILE + 1, c_at])
        total = [jnp.zeros((BS, BS), jnp.float32)] * 2
        for a in range(KAL):
            k = table[chunk * TILE, i * KAL + a] // 4
            a_high, a_low = split(block(a_v, (chunk * ROWS + i) * KAL + a))
            b_high, b_low = split(jnp.concatenate((block(b_v, k), block(b_v, 4 * NB + k)), axis=1))
            product = jnp.dot(
                jnp.concatenate((a_high, a_low, a_high), axis=1),
                jnp.concatenate((b_high, b_high, b_low), axis=0),
                preferred_element_type=jnp.float32,
            )
            owner, j = k // NB, lax.rem(k, NB)
            for s in range(2):
                col = table[(4 + s * 4 + owner) * TILE, j]
                match = jnp.where(col == kept[s], 1.0, 0.0).astype(jnp.float32)
                total[s] = total[s] + match * product[:, s * BS:(s + 1) * BS]
        for s in range(2):
            c_v[chunk, s, i] = total[s]

    def place_of(d, s):
        out, at = routes[d, s]
        return outs[out].at[pl.ds(at, ROWS)]

    for chunk, (distance, kept_core) in enumerate(spans):
        there = lax.rem(z + jnp.where(co == kept_core, 8 - distance, distance), 8)
        chunks[chunk].wait()
        for i in range(ROWS):
            one_row(chunk, there, i)
        layer = lax.rem(there // 2 - y + 4, 4)
        for d in range(4):
            @pl.when(layer == d)
            def _(d=d, chunk=chunk):
                for s in range(2):
                    pltpu.make_async_copy(c_v.at[chunk, s], place_of(d, s), sems.at[3 + d * 2 + s]).start()
    for i in range(8):
        pltpu.make_async_copy(c_v.at[i // 2, i % 2], place_of(i // 2, i % 2), sems.at[3 + i]).wait()


def products(place, spans, routes, a_parts, b_parts):
    n = ROWS * KAL
    places = list(routes.values())
    out_rows = [ROWS + max(at for out, at in places if out == i) for i in range(1 + max(places)[0])]
    anywhere = pl.BlockSpec(memory_space=pl.ANY)
    far_memory = pl.BlockSpec(memory_space=pl.ANY)
    return pl.pallas_call(
        functools.partial(product_kernel, spans, routes, len(b_parts)),
        out_shape=[jax.ShapeDtypeStruct((rows, BS, BS), jnp.float32) for rows in out_rows],
        in_specs=[pl.BlockSpec(memory_space=pltpu.SMEM)]
        + [far_memory] * len(a_parts)
        + [far_memory] * len(b_parts),
        out_specs=[anywhere] * len(out_rows),
        scratch_shapes=[
            pltpu.VMEM((4 * n * BS, BS), jnp.float32),
            pltpu.VMEM((8 * NB * BS, BS), jnp.float32),
            pltpu.VMEM((4, 2, ROWS, BS, BS), jnp.float32),
            pltpu.VMEM((12 * TILE, BS), jnp.float32),
            pltpu.VMEM((12 * TILE, BS), jnp.int32),
            pltpu.SMEM((12 * TILE, BS), jnp.int32),
            pltpu.SemaphoreType.DMA((15,)),
        ],
        compiler_params=pltpu.CompilerParams(vmem_limit_bytes=58 * 1024 * 1024),
        cost_estimate=pl.CostEstimate(
            flops=8 * n * BS ** 3 * 6, bytes_accessed=(4 * n + 8 * NB + 8 * ROWS) * BS * BS * 4, transcendentals=0
        ),
    )(place, *a_parts, *b_parts)


def swap(value):
    return shift(value, "co", 2, 1)


def pass_on(value):
    at = lambda x, core: (x % 2) * 4 + core * 2 + x % 4 // 2
    pairs = [(at(x, core), at(x + 1 - 2 * core, core)) for x in range(4) for core in range(2)]
    return lax.ppermute(value, ("xl", "co", "xh"), pairs)


def pass_z(value):
    pairs = [(core * 8 + z, core * 8 + (z + 1 - 2 * core) % 8) for z in range(8) for core in range(2)]
    return lax.ppermute(value, ("co", "z"), pairs)


def gather(a, b):
    own, other = [a], [swap(a)]
    for _ in range(2):
        own.append(pass_z(own[-1]))
        other.append(pass_z(other[-1]))
    b_other = swap(b)
    near, near_other, own[2], other[2] = together(pass_on(b), pass_on(b_other), own[2], other[2])
    far = pass_on(near)
    own.append(pass_z(own[2]))
    other.append(pass_z(other[2]))
    last = pass_z(own[3])
    near, near_other, own[3] = together(near, near_other, own[3])
    far, own[3] = together(far, own[3])
    odd = (own[1], swap(other[1]), own[3], swap(other[3]))
    even = (a, own[2], swap(other[2]), last)
    return odd, even, [b, b_other, near, near_other, far, swap(near), swap(near_other), swap(far)]


def together(*values):
    return lax.optimization_barrier(values)


def up(value):
    return shift(value, "y", 4, 1)


def down(value):
    return shift(value, "y", 4, -1)


def per_device(a_blocks, a_inner, b_blocks, b_cols, c_cols):
    place = jnp.stack([lax.axis_index(name) for name in ("xl", "co", "z", "xh", "y")])
    odd, even, b_parts = gather(with_ids(a_blocks, a_inner), with_ids(b_blocks, b_cols, c_cols))
    p = products(place, ((1, 0), (1, 1), (3, 0), (3, 1)), PAIRED, odd, b_parts)
    p_up, p_down, p_0, p_1, p_near_0, p_near_1 = p
    p_up, p_down = up(p_up), down(p_down)
    q = products(place, ((0, 0), (2, 0), (2, 1), (4, 0)), SINGLE, even, b_parts)
    p_up, p_down, _ = together(p_up, p_down, q[0])
    p_near_0, p_near_1 = up(p_near_0 + p_up[:ROWS]), down(p_near_1 + p_down[:ROWS])
    q_far_1, q_plain_1, q_far_0 = down(q[5]), up(q[3]), up(q[4])
    q7, q6, q_far_1 = together(q[7], q[6], q_far_1)
    p_other = shift(p_1 + p_up[ROWS:] + p_near_1, "xh", 2, 1)
    q_near_1, q_plain_0 = down(q7 + q_far_1), down(q6)
    q_other = shift(q[1] + q_plain_1 + q_near_1, "xh", 2, 1)
    q_far_0, p_near_0 = together(q_far_0, p_near_0)
    q_near_0 = up(q[2] + q_far_0)
    p_mine = p_0 + p_near_0 + p_down[ROWS:]
    q_mine = q[0] + q_near_0 + q_plain_0
    own_parity = lax.axis_index("z") % 2
    own_half = lax.axis_index("xh")
    rows = []
    for parity in range(2):
        mine = jnp.where(own_parity == parity, q_mine, p_mine)
        other = jnp.where(own_parity == parity, q_other, p_other)
        rows += [jnp.where(own_half == 0, mine, other), jnp.where(own_half == 0, other, mine)]
    return jnp.stack(rows).reshape(4 * ROWS, 1, BS, BS)


def solution(mesh):
    fine = Mesh(mesh.devices.reshape(2, 2, 8, 2, 4), ("xl", "co", "z", "xh", "y"))
    return jax.shard_map(
        per_device,
        mesh=fine,
        in_specs=(
            P(("xl", "co", "z", "xh"), "y", None, None),
            P(("xl", "co", "z", "xh"), "y"),
            P(("xl", "co"), "y", ("z", "xh"), None, None),
            P(("xl", "co"), "y", ("z", "xh")),
            P(("xl", "co"), ("z", "xh")),
        ),
        out_specs=P(("xl", "co", "y"), ("z", "xh"), None, None),
        check_vma=False,
    )
```
